32 devices in a mesh: lat: 8 (over z, y), lon: 4 (over x, core).
Axes of the slice: x: 2, y: 2, z: 4, core: 2. Of those that a mesh axis runs over, the one named last changes fastest.
Arguments:
- meridian_slab_data: bfloat16 [256, 96, 1024], P('lat', None, 'lon'), may hold values from -6 to 6
- smoothing_filter_taps: bfloat16 [3, 3, 96, 128], replicated, may hold values from -0.21875 to 0.21875
- smoothing_offset_entries: float32 [128], replicated, may hold values from -3 to 3
- opening_coarsen_taps: bfloat16 [4, 4, 128, 256], replicated, may hold values from -0.125 to 0.125
- opening_coarsen_offset: float32 [256], replicated, may hold values from -3 to 3
- closing_coarsen_taps: bfloat16 [4, 4, 256, 256], replicated, may hold values from -0.09375 to 0.09375
- closing_coarsen_offset: float32 [256], replicated, may hold values from -3 to 3
- layernorm_multiplier: float32 [256], replicated, may hold values from 0.25 to 1.75
- triple_mapping_matrix: bfloat16 [256, 768], replicated, may hold values from -0.375 to 0.375
- logit_sharpness: float32 [8], replicated, may hold values from 2.5 to 40, as said below
- mixing_return_matrix: bfloat16 [256, 256], replicated, may hold values from -0.375 to 0.375
Outputs:
- encoded: bfloat16 [64, 256, 256], P('lat', 'lon')
The draws below stay inside these ranges and needn't reach their ends.
Inputs may be any that keep to these rules, and one draw needn't show every extreme that they name: `logit_sharpness`: per-head score scales.
All inputs are finite; a program needn't handle non-finite values.
Results may differ from the reference program's by a relative error of at most 0.034.
Values may be sent and summed in bfloat16 or wider, within the bound.
A program may use at most 128 MiB of HBM per device.

```python
import jax
import jax.numpy as jnp
from jax import lax

CIN = 96
PRIMARY_CHANS = 128
REDUCED_CHANS = 256
HEADS = 8
LAT = 256
LON = 1024


def draw_logit_sharpness(key, part):
    base = jax.random.uniform(key, (HEADS,), jnp.float32, 2.5, 8.0)
    return base


def level_of(stream_key, dims, shards, least, largest):
    gain = 1.0
    for position, parts in shards:
        draws = jax.random.uniform(jax.random.fold_in(jax.random.fold_in(stream_key, 6), position), (parts,), jnp.float32, least / len(shards), largest / len(shards))
        gain = gain * jnp.repeat(jnp.exp(draws), dims[position] // parts).reshape((-1,) + (1,) * (len(dims) - 1 - position))
    return gain


def scatter_about(key, shape, scale, bound, pieces=(), kind=jnp.bfloat16):
    entries = jax.random.normal(key, shape, jnp.float32) * scale
    if len(pieces) > 0:
        entries = level_of(key, shape, pieces, -0.22, 0.18) * entries
    return jnp.clip(entries, min=-bound, max=bound).astype(kind)


def setup_inputs(seed: int = 0) -> dict:
    keys = jax.random.split(jax.random.key(seed), 12)
    return {
        "meridian_slab_data": scatter_about(keys[0], (LAT, CIN, LON), 1.0, 6.0, ((0, 8), (2, 4))),
        "smoothing_filter_taps": scatter_about(keys[1], (3, 3, CIN, PRIMARY_CHANS), (9 * CIN) ** -0.5, 0.21875),
        "smoothing_offset_entries": scatter_about(keys[2], (PRIMARY_CHANS,), 0.5, 3.0, (), jnp.float32),
        "opening_coarsen_taps": scatter_about(keys[3], (4, 4, PRIMARY_CHANS, REDUCED_CHANS), (16 * PRIMARY_CHANS) ** -0.5, 0.125),
        "opening_coarsen_offset": scatter_about(keys[4], (REDUCED_CHANS,), 0.5, 3.0, (), jnp.float32),
        "closing_coarsen_taps": scatter_about(keys[5], (4, 4, REDUCED_CHANS, REDUCED_CHANS), (16 * REDUCED_CHANS) ** -0.5, 0.09375),
        "closing_coarsen_offset": scatter_about(keys[6], (REDUCED_CHANS,), 0.5, 3.0, (), jnp.float32),
        "layernorm_multiplier": jnp.clip(1.0 + 0.15 * jax.random.normal(keys[7], (REDUCED_CHANS,), jnp.float32), 0.25, 1.75),
        "triple_mapping_matrix": scatter_about(keys[8], (REDUCED_CHANS, 3 * REDUCED_CHANS), REDUCED_CHANS ** -0.5, 0.375),
        "logit_sharpness": draw_logit_sharpness(jax.random.fold_in(keys[11], 71), 0),
        "mixing_return_matrix": scatter_about(keys[10], (REDUCED_CHANS, REDUCED_CHANS), REDUCED_CHANS ** -0.5, 0.375),
    }


def pad_grid(values):
    wrapped = jnp.concatenate([values[:, -1:], values, values[:, :1]], axis=1)
    return jnp.pad(wrapped, ((1, 1), (0, 0), (0, 0)))

def apply_filter(values, kernel, bias, stride):
    padded = pad_grid(values).astype(jnp.float32)
    total = lax.conv_general_dilated(padded[None], kernel.astype(jnp.float32), (stride, stride), 'VALID', dimension_numbers=('NHWC', 'HWIO', 'NHWC'), precision=lax.Precision.HIGHEST)[0]
    return jax.nn.silu(total + bias).astype(jnp.bfloat16)

def reference(meridian_slab_data, smoothing_filter_taps, smoothing_offset_entries, opening_coarsen_taps, opening_coarsen_offset, closing_coarsen_taps, closing_coarsen_offset, layernorm_multiplier, triple_mapping_matrix, logit_sharpness, mixing_return_matrix):
    channels_last = jnp.transpose(meridian_slab_data, (0, 2, 1))
    opening_halved = apply_filter(channels_last, smoothing_filter_taps, smoothing_offset_entries, 1)
    closing_halved = apply_filter(opening_halved, opening_coarsen_taps, opening_coarsen_offset, 2)
    activation_maps = apply_filter(closing_halved, closing_coarsen_taps, closing_coarsen_offset, 2)
    widths = activation_maps.shape[2]
    per_group_channel_count = widths // HEADS
    upcast = activation_maps.astype(jnp.float32)
    mean = lax.optimization_barrier(jnp.mean(upcast, axis=-1, keepdims=True))
    centred = upcast - mean
    variance = lax.optimization_barrier(jnp.mean(centred * centred, axis=-1, keepdims=True))
    normed = (centred * lax.rsqrt(variance + 1e-05) * layernorm_multiplier).astype(jnp.bfloat16)
    projected = jnp.einsum('rtc,cf->rtf', normed.astype(jnp.float32), triple_mapping_matrix.astype(jnp.float32), precision=lax.Precision.HIGHEST)
    shape = (activation_maps.shape[0], activation_maps.shape[1], HEADS, per_group_channel_count)
    logit_multiplier = (logit_sharpness / jnp.sqrt(jnp.float32(per_group_channel_count)))[:, None]
    query = (projected[..., :widths].reshape(shape) * logit_multiplier).astype(jnp.bfloat16)
    key = projected[..., widths:2 * widths].reshape(shape).astype(jnp.bfloat16)
    value = projected[..., 2 * widths:].reshape(shape).astype(jnp.bfloat16)

    def one_row(trio):
        row_query, row_key, row_value = trio
        scores = jnp.einsum('shd,thd->hst', row_query.astype(jnp.float32), row_key.astype(jnp.float32), precision=lax.Precision.HIGHEST)
        best = lax.optimization_barrier(jnp.max(scores, axis=-1, keepdims=True))
        weights = jnp.exp(scores - best)
        total = lax.optimization_barrier(jnp.sum(weights, axis=-1))
        rounded = weights.astype(jnp.bfloat16).astype(jnp.float32)
        summed = jnp.einsum('hst,thd->shd', rounded, row_value.astype(jnp.float32), precision=lax.Precision.HIGHEST)
        return (summed / jnp.transpose(total)[:, :, None]).astype(jnp.bfloat16)
    attended = lax.map(one_row, (query, key, value)).reshape(activation_maps.shape)
    mixed = jnp.einsum('rtc,cf->rtf', attended.astype(jnp.float32), mixing_return_matrix.astype(jnp.float32), precision=lax.Precision.HIGHEST)
    return (upcast + mixed).astype(jnp.bfloat16)
```

```python
import functools

import jax
import jax.numpy as jnp
from jax import lax
from jax.experimental import pallas as pl
from jax.experimental.pallas import tpu as pltpu
from jax.sharding import PartitionSpec as P

HEADS = 8
HALO = 4
BF = jnp.bfloat16
F32 = jnp.float32


def silu(v):
    half = 0.5 * v
    return half + half * jnp.tanh(half)


def dot(a, b):
    return jnp.dot(a, b, preferred_element_type=F32)


def build_first_kernel(taps_ref, w1):
    cin, cout = taps_ref.shape[2:]
    w1[...] = jnp.zeros_like(w1)
    for dy in range(3):
        for col in range(4):
            for out in range(2):
                if 0 <= col - out < 3:
                    w1[dy, col * 128 : col * 128 + cin, out * cout : (out + 1) * cout] = taps_ref[
                        dy, col - out
                    ]


def spread_row(value, left, right, xt, slot, xa, row, wide):
    cin, cols = value.shape
    xt[slot, HALO : HALO + cols, 0:cin] = value.astype(F32).T
    xt[slot, 0:HALO, :] = left.astype(F32)
    xt[slot, HALO + cols : 2 * HALO + cols, :] = right.astype(F32)
    for phase in range(6):
        part = xt[slot, pl.ds(phase, wide, 4), :]
        xa[pl.ds(row * wide, wide), phase * 128 : (phase + 1) * 128] = part.astype(BF)


def conv_kernel(
    wide, x_ref, top_ref, bottom_ref, left_ref, right_ref, taps_ref, b1_ref, w2_ref, b2_ref, w3_ref,
    b3_ref, out_ref, w1, xt, xa, first, second,
):
    lat = lax.axis_index("lat")
    bands = lax.axis_size("lat")
    rows, cin, cols = x_ref.shape
    tokens = cols // 4
    build_first_kernel(taps_ref, w1)
    xt[...] = jnp.zeros_like(xt)

    def own(step, carry):
        for k in range(4):
            r = step * 4 + k
            spread_row(
                x_ref[r], left_ref[r + HALO], right_ref[r + HALO], xt, k, xa, r + HALO, wide
            )
        return carry

    lax.fori_loop(0, rows // 4, own, 0)
    for k in range(HALO):
        spread_row(top_ref[k], left_ref[k], right_ref[k], xt, k, xa, k, wide)
    for k in range(HALO):
        r = rows + HALO + k
        spread_row(bottom_ref[k], left_ref[r], right_ref[r], xt, k, xa, r, wide)

    @pl.when(lat == 0)
    def _():
        xa[0 : HALO * wide, :] = jnp.zeros((HALO * wide, xa.shape[1]), BF)

    @pl.when(lat == bands - 1)
    def _():
        xa[(rows + HALO) * wide :, :] = jnp.zeros((HALO * wide, xa.shape[1]), BF)

    bias1 = jnp.concatenate([b1_ref[...], b1_ref[...]], axis=1)

    def conv1(step, carry):
        pair = []
        for side in range(2):
            total = bias1
            for dy in range(3):
                lhs = xa[
                    pl.ds((2 * step + dy) * wide, 2 * wide), side * 256 : side * 256 + 512
                ]
                total = total + dot(lhs, w1[dy])
            pair.append(silu(total))
        for k in range(2):
            row = lat * rows + 2 * step + k - 3
            inside = (row >= 0) & (row < bands * rows)
            where = pl.ds(step * wide, wide)
            a = jnp.where(inside, pair[0][k * wide : (k + 1) * wide], 0.0)
            b = jnp.where(inside, pair[1][k * wide : (k + 1) * wide], 0.0)
            first[k, where, 0:256] = a.astype(BF)
            first[k, where, 256:512] = b.astype(BF)
            first[k, where, 512:768] = pltpu.roll(a, wide - 1, 0).astype(BF)
        return carry

    lax.fori_loop(0, (rows + 6) // 2, conv1, 0)

    half = rows // 2

    def conv2(step, carry):
        sides = []
        for side in range(2):
            total = b2_ref[...]
            for dy in range(4):
                lhs = first[
                    dy % 2,
                    pl.ds((2 * step + dy // 2) * wide, 2 * wide),
                    side * 256 : side * 256 + 512,
                ]
                total = total + dot(lhs, w2_ref[dy])
            sides.append(silu(total))
        for k in range(2):
            row = lat * half + 2 * step + k - 1
            inside = (row >= 0) & (row < bands * half)
            where = pl.ds(step * tokens, tokens)
            for side in range(2):
                a = jnp.where(inside, sides[side][k * wide : (k + 1) * wide], 0.0)
                second[k, where, side * 256 : side * 256 + 256] = a[:tokens].astype(BF)
                second[k, where, 512 + side * 256 : 768 + side * 256] = pltpu.roll(
                    a, wide - 1, 0
                )[:tokens].astype(BF)
        return carry

    lax.fori_loop(0, (half + 2) // 2, conv2, 0)

    final = rows // 4
    part = final // 2

    def conv3(step, carry):
        total = b3_ref[...]
        for dy in range(4):
            lhs = second[dy % 2, pl.ds((step * part + dy // 2) * tokens, part * tokens), :]
            total = total + dot(lhs, w3_ref[dy])
        out_ref[pl.ds(step * part, part)] = (
            silu(total).astype(BF).reshape(part, tokens, total.shape[1])
        )
        return carry

    lax.fori_loop(0, 2, conv3, 0)


def attention_kernel(f_ref, gain_ref, wqkv_ref, sharp_ref, wo_ref, out_ref, qs, ks, vs, att):
    rows, tokens, width = f_ref.shape
    depth = width // HEADS
    feats = f_ref[...].reshape(rows * tokens, width).astype(F32)
    mean = jnp.mean(feats, axis=-1, keepdims=True)
    centred = feats - mean
    variance = jnp.mean(centred * centred, axis=-1, keepdims=True)
    normed = (centred * lax.rsqrt(variance + 1e-05) * gain_ref[...]).astype(BF)
    lane = lax.broadcasted_iota(jnp.int32, (1, width), 1)
    scale = jnp.zeros((1, width), F32)
    for h in range(HEADS):
        mine = (lane >= h * depth) & (lane < (h + 1) * depth)
        scale = jnp.where(mine, sharp_ref[h] / jnp.sqrt(F32(depth)), scale)
    qs[...] = (dot(normed, wqkv_ref[:, :width]) * scale).astype(BF)
    ks[...] = dot(normed, wqkv_ref[:, width : 2 * width]).astype(BF)
    vs[...] = dot(normed, wqkv_ref[:, 2 * width :]).astype(BF)
    block = min(256, tokens)
    per_row = tokens // block

    def body(step, carry):
        row = step // per_row
        q = qs[pl.ds(step * block, block), :]
        k = ks[pl.ds(row * tokens, tokens), :]
        v = vs[pl.ds(row * tokens, tokens), :]
        joined = jnp.zeros((block, width), F32)
        for h in range(HEADS):
            mine = (lane >= h * depth) & (lane < (h + 1) * depth)
            masked = jnp.where(mine, q.astype(F32), 0.0).astype(BF)
            scores = lax.dot_general(
                masked, k, (((1,), (1,)), ((), ())), preferred_element_type=F32
            )
            weights = jnp.exp(scores - jnp.max(scores, axis=-1, keepdims=True))
            total = jnp.sum(weights, axis=-1, keepdims=True)
            summed = dot(weights.astype(BF), v)
            joined = jnp.where(mine, summed / total, joined)
        att[pl.ds(step * block, block), :] = joined.astype(BF)
        return carry

    lax.fori_loop(0, rows * per_row, body, 0)
    mixed = dot(att[...], wo_ref[...])
    out_ref[...] = (feats + mixed).astype(BF).reshape(rows, tokens, width)


VM = pl.BlockSpec(memory_space=pltpu.VMEM)
SM = pl.BlockSpec(memory_space=pltpu.SMEM)


def on_device(x, taps1, b1, taps2, b2, taps3, b3, gain, wqkv, sharp, wo):
    rows, cin, cols = x.shape
    tokens = cols // 4
    bands, sectors = lax.axis_size("lat"), lax.axis_size("lon")
    width = taps3.shape[3]
    wide = -(-(tokens + 2) // 16) * 16

    def ring(axis, size, last, initial):
        up = [(i, (i + 1) % size) for i in range(size)]
        down = [(j, i) for i, j in up]
        return lax.ppermute(last, axis, up), lax.ppermute(initial, axis, down)

    top, bottom = ring("lat", bands, x[-HALO:], x[:HALO])

    def edge(a):
        b = jnp.concatenate([top[:, :, a], x[:, :, a], bottom[:, :, a]], axis=0)
        return jnp.pad(jnp.transpose(b, (0, 2, 1)), ((0, 0), (0, 0), (0, 128 - cin)))

    left, right = ring("lon", sectors, edge(slice(cols - HALO, cols)), edge(slice(0, HALO)))
    features = pl.pallas_call(
        functools.partial(conv_kernel, wide),
        out_shape=jax.ShapeDtypeStruct((rows // 4, tokens, width), BF),
        in_specs=[VM] * 11,
        out_specs=VM,
        scratch_shapes=[
            pltpu.VMEM((3, 512, 256), BF),
            pltpu.VMEM((4, 4 * wide + 8, 128), F32),
            pltpu.VMEM(((rows + 2 * HALO) * wide, 768), BF),
            pltpu.VMEM((2, (rows + 6) // 2 * wide, 768), BF),
            pltpu.VMEM((2, (rows // 2 + 2) // 2 * tokens, 1024), BF),
        ],
        compiler_params=pltpu.CompilerParams(vmem_limit_bytes=56 * 2**20),
        name="convs",
    )(
        x, top, bottom, left, right, taps1, b1[None], taps2.reshape(4, -1, width), b2[None],
        taps3.reshape(4, -1, width), b3[None],
    )
    copies = max(1, sectors // features.shape[0])
    if copies > 1:
        features = jnp.repeat(features, copies, axis=0)
    whole_rows = lax.all_to_all(features, "lon", 0, 1, tiled=True)
    n = whole_rows.shape[0] * whole_rows.shape[1]
    encoded = pl.pallas_call(
        attention_kernel,
        out_shape=jax.ShapeDtypeStruct(whole_rows.shape, BF),
        in_specs=[VM, VM, VM, SM, VM],
        out_specs=VM,
        scratch_shapes=[pltpu.VMEM((n, width), BF)] * 4,
        compiler_params=pltpu.CompilerParams(vmem_limit_bytes=56 * 2**20),
        name="attention",
    )(whole_rows, gain[None], wqkv, sharp, wo)
    return lax.all_to_all(encoded, "lon", 1, 0, tiled=True)[::copies]


def solution(mesh):
    return jax.shard_map(
        on_device,
        mesh=mesh,
        in_specs=(P("lat", None, "lon"), P(), P(), P(), P(), P(), P(), P(), P(), P(), P()),
        out_specs=P("lat", "lon", None),
        check_vma=False,
    )
```

```python
import functools

import jax
import jax.numpy as jnp
from jax import lax
from jax.experimental import pallas as pl
from jax.experimental.pallas import tpu as pltpu
from jax.sharding import PartitionSpec as P

HEADS = 8
HALO = 4
BF = jnp.bfloat16
F32 = jnp.float32


def silu(v):
    half = 0.5 * v
    return half + half * jnp.tanh(half)


def dot(a, b):
    return jnp.dot(a, b, preferred_element_type=F32)


def build_first_kernel(taps_ref, w1):
    cin, cout = taps_ref.shape[2:]
    w1[...] = jnp.zeros_like(w1)
    for dy in range(3):
        for col in range(4):
            for out in range(2):
                if 0 <= col - out < 3:
                    w1[dy, col * 128 : col * 128 + cin, out * cout : (out + 1) * cout] = taps_ref[
                        dy, col - out
                    ]


def turned(value):
    cin, cols = value.shape
    zeros = jnp.zeros((128 - cin, cols), F32)
    return jnp.concatenate([value.astype(F32), zeros], axis=0).T


def remote(src, dst, send, recv, lat, lon):
    return pltpu.make_async_remote_copy(
        src_ref=src, dst_ref=dst, send_sem=send, recv_sem=recv, device_id=(lat, lon),
        device_id_type=pl.DeviceIdType.MESH,
    )


def kernel(
    wide, x_ref, taps_ref, b1_ref, w2_hbm, b2_ref, w3_hbm, b3_ref, gain_ref, wqkv_hbm, sharp_ref,
    wo_hbm, out_ref, w2_ref, w3_ref, wqkv_ref, wo_ref, w1, top, bottom, edges, rims, xt, xa, first,
    second, local, whole, qs, ks, vs, att, enc, landed, weight_sem, row_sem, edge_send, edge_recv,
    go_send, go_recv, back_send, back_recv,
):
    lat, lon = lax.axis_index("lat"), lax.axis_index("lon")
    bands, sectors = lax.axis_size("lat"), lax.axis_size("lon")
    rows, cin, cols = x_ref.shape
    tokens = cols // 4
    groups = rows // 4
    has_up, has_down = lat > 0, lat < bands - 1
    up, down = jnp.maximum(lat - 1, 0), jnp.minimum(lat + 1, bands - 1)
    west, east = lax.rem(lon + sectors - 1, sectors), lax.rem(lon + 1, sectors)
    both = ((has_up, up), (has_down, down))

    weights = [
        pltpu.make_async_copy(src, dst, weight_sem.at[i])
        for i, (src, dst) in enumerate(
            ((w2_hbm, w2_ref), (w3_hbm, w3_ref), (wqkv_hbm, wqkv_ref), (wo_hbm, wo_ref))
        )
    ]

    barrier = pltpu.get_barrier_semaphore()

    def greet(to_lat, to_lon):
        pl.semaphore_signal(
            barrier, inc=1, device_id=(to_lat, to_lon), device_id_type=pl.DeviceIdType.MESH
        )

    for step in range(1, sectors):
        greet(lat, lax.rem(lon + step, sectors))
    for there, other in both:
        @pl.when(there)
        def _():
            greet(other, lon)
            greet(other, west)
            greet(other, east)

    for copy in weights:
        copy.start()
    build_first_kernel(taps_ref, w1)
    for r in range(rows + 2 * HALO):
        xt[r, 2 * HALO + cols :, :] = jnp.zeros((xt.shape[1] - cols - 2 * HALO, 128), F32)

    peers = sectors - 1 + jnp.where(has_up, 3, 0) + jnp.where(has_down, 3, 0)
    pl.semaphore_wait(barrier, peers)

    to_up = remote(x_ref.at[0:HALO], bottom, row_sem.at[0], row_sem.at[2], up, lon)
    to_down = remote(
        x_ref.at[rows - HALO : rows], top, row_sem.at[1], row_sem.at[3], down, lon
    )

    @pl.when(has_up)
    def _():
        to_up.start()

    @pl.when(has_down)
    def _():
        to_down.start()

    def own(step, carry):
        initial, last = [], []
        for k in range(4):
            r = step * 4 + k
            value = turned(x_ref[r])
            xt[r + HALO, HALO : HALO + cols, :] = value
            initial.append(value[:HALO])
            last.append(value[cols - HALO :])
        edges[0, step] = jnp.concatenate(initial, axis=0).astype(BF)
        edges[1, step] = jnp.concatenate(last, axis=0).astype(BF)
        return carry

    lax.fori_loop(0, groups, own, 0)

    rim_copies = []
    for side, to_lon in ((0, west), (1, east)):
        slot = 3 * side
        target = 1 - side
        rim_copies.append(
            (None, None, remote(
                edges.at[side], rims.at[target, pl.ds(1, groups)], edge_send.at[slot],
                edge_recv.at[slot], lat, to_lon,
            ))
        )
        rim_copies.append(
            (has_up, has_down, remote(
                edges.at[side, 0], rims.at[target, groups + 1], edge_send.at[slot + 1],
                edge_recv.at[slot + 1], up, to_lon,
            ))
        )
        rim_copies.append(
            (has_down, has_up, remote(
                edges.at[side, groups - 1], rims.at[target, 0], edge_send.at[slot + 2],
                edge_recv.at[slot + 2], down, to_lon,
            ))
        )

    def run(condition, act):
        if condition is None:
            act()
        else:
            pl.when(condition)(act)

    for sends, _, copy in rim_copies:
        run(sends, copy.start)

    @pl.when(has_up)
    def _():
        to_down.wait_recv()
        for k in range(HALO):
            xt[k, HALO : HALO + cols, :] = turned(top[k])

    @pl.when(has_down)
    def _():
        to_up.wait_recv()
        for k in range(HALO):
            xt[rows + HALO + k, HALO : HALO + cols, :] = turned(bottom[k])

    for _, receives, copy in rim_copies:
        run(receives, copy.wait_recv)

    def spread(step, carry):
        left = rims[0, step].astype(F32)
        right = rims[1, step].astype(F32)
        for k in range(4):
            r = step * 4 + k
            xt[r, 0:HALO, :] = left[k * HALO : (k + 1) * HALO]
            xt[r, HALO + cols : 2 * HALO + cols, :] = right[k * HALO : (k + 1) * HALO]
            for phase in range(6):
                part = xt[r, pl.ds(phase, wide, 4), :]
                xa[pl.ds(r * wide, wide), phase * 128 : (phase + 1) * 128] = part.astype(BF)
        return carry

    low = jnp.where(has_up, 0, 1)
    high = jnp.where(has_down, groups + 2, groups + 1)
    lax.fori_loop(low, high, spread, 0)

    @pl.when(lat == 0)
    def _():
        xa[0 : HALO * wide, :] = jnp.zeros((HALO * wide, xa.shape[1]), BF)

    @pl.when(lat == bands - 1)
    def _():
        xa[(rows + HALO) * wide :, :] = jnp.zeros((HALO * wide, xa.shape[1]), BF)

    bias1 = jnp.concatenate([b1_ref[...], b1_ref[...]], axis=1)

    def conv1(step, carry):
        pair = []
        for side in range(2):
            total = bias1
            for dy in range(3):
                lhs = xa[
                    pl.ds((2 * step + dy) * wide, 2 * wide), side * 256 : side * 256 + 512
                ]
                total = total + dot(lhs, w1[dy])
            pair.append(silu(total))
        for k in range(2):
            row = lat * rows + 2 * step + k - 3
            inside = (row >= 0) & (row < bands * rows)
            where = pl.ds(step * wide, wide)
            a = jnp.where(inside, pair[0][k * wide : (k + 1) * wide], 0.0)
            b = jnp.where(inside, pair[1][k * wide : (k + 1) * wide], 0.0)
            first[k, where, 0:256] = a.astype(BF)
            first[k, where, 256:512] = b.astype(BF)
            first[k, where, 512:768] = pltpu.roll(a, wide - 1, 0).astype(BF)
        return carry

    lax.fori_loop(0, (rows + 6) // 2, conv1, 0)

    half = rows // 2
    weights[0].wait()

    def conv2(step, carry):
        sides = []
        for side in range(2):
            total = b2_ref[...]
            for dy in range(4):
                lhs = first[
                    dy % 2,
                    pl.ds((2 * step + dy // 2) * wide, 2 * wide),
                    side * 256 : side * 256 + 512,
                ]
                total = total + dot(lhs, w2_ref[dy])
            sides.append(silu(total))
        for k in range(2):
            row = lat * half + 2 * step + k - 1
            inside = (row >= 0) & (row < bands * half)
            where = pl.ds(step * tokens, tokens)
            for side in range(2):
                a = jnp.where(inside, sides[side][k * wide : (k + 1) * wide], 0.0)
                second[k, where, side * 256 : side * 256 + 256] = a[:tokens].astype(BF)
                second[k, where, 512 + side * 256 : 768 + side * 256] = pltpu.roll(
                    a, wide - 1, 0
                )[:tokens].astype(BF)
        return carry

    lax.fori_loop(0, (half + 2) // 2, conv2, 0)

    final = rows // 4
    parts = 2
    part = final // parts
    copies = max(1, sectors // final)
    each = max(1, final // sectors)
    width = w3_ref.shape[2]
    long = sectors * tokens
    share = long // copies
    weights[1].wait()

    def go(peer):
        begin = peer // copies * each
        return remote(
            local.at[pl.ds(begin, each)],
            whole.at[:, pl.ds(lon * tokens, tokens)],
            go_send.at[peer], go_recv.at[lon], lat, peer,
        )

    for step in range(parts):
        total = b3_ref[...]
        for dy in range(4):
            begin = (step * part + dy // 2) * tokens
            lhs = second[dy % 2, begin : begin + part * tokens, :]
            total = total + dot(lhs, w3_ref[dy])
        local[step * part : (step + 1) * part] = (
            silu(total).astype(BF).reshape(part, tokens, width)
        )
        for peer in range(sectors):
            if (peer // copies * each) // part == step:
                @pl.when(lon != peer)
                def _():
                    go(peer).start()

    mine_at = lon // copies * each
    whole[:, pl.ds(pl.multiple_of(lon * tokens, tokens), tokens), :] = local[
        pl.ds(mine_at, each)
    ]
    weights[2].wait()
    weights[3].wait()
    for peer in range(sectors):
        @pl.when(lon != peer)
        def _():
            remote(
                local.at[pl.ds(0, each)], whole.at[:, peer * tokens : (peer + 1) * tokens],
                go_send.at[peer], go_recv.at[peer], lat, peer,
            ).wait_recv()

    depth = width // HEADS
    lane = lax.broadcasted_iota(jnp.int32, (1, width), 1)
    scale = jnp.zeros((1, width), F32)
    for h in range(HEADS):
        inside = (lane >= h * depth) & (lane < (h + 1) * depth)
        scale = jnp.where(inside, sharp_ref[h] / jnp.sqrt(F32(depth)), scale)
    block = min(256, share)
    query_at = lax.rem(lon, copies) * share

    def back(i, peer, src_at):
        return remote(
            enc.at[i, pl.ds(src_at, tokens)], landed.at[lon // copies * each + i],
            back_send.at[i, peer], back_recv.at[i, lon], lat, peer,
        )

    for i in range(each):
        feats = whole[i].astype(F32)
        mean = jnp.mean(feats, axis=-1, keepdims=True)
        centred = feats - mean
        variance = jnp.mean(centred * centred, axis=-1, keepdims=True)
        normed = (centred * lax.rsqrt(variance + 1e-05) * gain_ref[...]).astype(BF)
        qs[i] = (dot(normed, wqkv_ref[:, :width]) * scale).astype(BF)
        ks[i] = dot(normed, wqkv_ref[:, width : 2 * width]).astype(BF)
        vs[i] = dot(normed, wqkv_ref[:, 2 * width :]).astype(BF)
        k = ks[i]
        v = vs[i]

        def attend(step, carry):
            at = pl.multiple_of(query_at + step * block, block)
            q = qs[i, pl.ds(at, block), :]
            joined = jnp.zeros((block, width), F32)
            for h in range(HEADS):
                inside = (lane >= h * depth) & (lane < (h + 1) * depth)
                masked = jnp.where(inside, q.astype(F32), 0.0).astype(BF)
                scores = lax.dot_general(
                    masked, k, (((1,), (1,)), ((), ())), preferred_element_type=F32
                )
                raised = jnp.exp(scores - jnp.max(scores, axis=-1, keepdims=True))
                total = jnp.sum(raised, axis=-1, keepdims=True)
                summed = dot(raised.astype(BF), v)
                joined = jnp.where(inside, summed / total, joined)
            mixed = dot(joined.astype(BF), wo_ref[...])
            res = whole[i, pl.ds(at, block), :].astype(F32)
            enc[i, pl.ds(at, block), :] = (res + mixed).astype(BF)
            return carry

        if share == block:
            attend(0, 0)
        else:
            lax.fori_loop(0, share // block, attend, 0)
        for peer in range(sectors):
            @pl.when((lon != peer) & (lax.rem(lon, copies) == peer * copies // sectors))
            def _():
                back(i, peer, peer * tokens).start()

        @pl.when(lax.rem(lon, copies) == lon * copies // sectors)
        def _():
            landed[lon // copies * each + i] = enc[
                i, pl.ds(pl.multiple_of(lon * tokens, tokens), tokens), :
            ]

    for i in range(each):
        for peer in range(sectors):
            @pl.when((lon != peer) & (lon * copies // sectors == peer % copies))
            def _():
                remote(
                    enc.at[i, 0:tokens], landed.at[peer // copies * each + i],
                    back_send.at[i, peer], back_recv.at[i, peer], lat, peer,
                ).wait_recv()
    out_ref[...] = landed[...]

    for sends, copy in ((has_up, to_up), (has_down, to_down)):
        run(sends, copy.wait_send)
    for sends, _, copy in rim_copies:
        run(sends, copy.wait_send)
    for peer in range(sectors):
        @pl.when(lon != peer)
        def _():
            go(peer).wait_send()
    for i in range(each):
        for peer in range(sectors):
            @pl.when((lon != peer) & (lax.rem(lon, copies) == peer * copies // sectors))
            def _():
                back(i, peer, peer * tokens).wait_send()


VM = pl.BlockSpec(memory_space=pltpu.VMEM)
SM = pl.BlockSpec(memory_space=pltpu.SMEM)
HB = pl.BlockSpec(memory_space=pl.ANY)


def on_device(x, taps1, b1, taps2, b2, taps3, b3, gain, wqkv, sharp, wo):
    rows, cin, cols = x.shape
    tokens = cols // 4
    sectors = lax.axis_size("lon")
    width = taps3.shape[3]
    wide = -(-(tokens + 2) // 16) * 16
    final = rows // 4
    each = max(1, final // sectors)
    long = sectors * tokens
    w2 = taps2.reshape(4, -1, width)
    w3 = taps3.reshape(4, -1, width)
    dma = pltpu.SemaphoreType.DMA
    return pl.pallas_call(
        functools.partial(kernel, wide),
        out_shape=jax.ShapeDtypeStruct((final, tokens, width), BF),
        in_specs=[VM, VM, VM, HB, VM, HB, VM, VM, HB, SM, HB],
        out_specs=VM,
        scratch_shapes=[
            pltpu.VMEM(w2.shape, BF),
            pltpu.VMEM(w3.shape, BF),
            pltpu.VMEM(wqkv.shape, BF),
            pltpu.VMEM(wo.shape, BF),
            pltpu.VMEM((3, 512, 256), BF),
            pltpu.VMEM((HALO, cin, cols), BF),
            pltpu.VMEM((HALO, cin, cols), BF),
            pltpu.VMEM((2, rows // 4, 16, 128), BF),
            pltpu.VMEM((2, rows // 4 + 2, 16, 128), BF),
            pltpu.VMEM((rows + 2 * HALO, 4 * wide + 8, 128), F32),
            pltpu.VMEM(((rows + 2 * HALO) * wide, 768), BF),
            pltpu.VMEM((2, (rows + 6) // 2 * wide, 768), BF),
            pltpu.VMEM((2, (rows // 2 + 2) // 2 * tokens, 1024), BF),
            pltpu.VMEM((final, tokens, width), BF),
        ]
        + [pltpu.VMEM((each, long, width), BF)] * 6
        + [
            pltpu.VMEM((final, tokens, width), BF),
            dma((4,)),
            dma((4,)),
            dma((6,)),
            dma((6,)),
            dma((sectors,)),
            dma((sectors,)),
            dma((each, sectors)),
            dma((each, sectors)),
        ],
        compiler_params=pltpu.CompilerParams(
            vmem_limit_bytes=60 * 2**20, collective_id=0, has_side_effects=True
        ),
        name="encoder",
    )(x, taps1, b1[None], w2, b2[None], w3, b3[None], gain[None], wqkv, sharp, wo)


def solution(mesh):
    return jax.shard_map(
        on_device,
        mesh=mesh,
        in_specs=(P("lat", None, "lon"), P(), P(), P(), P(), P(), P(), P(), P(), P(), P()),
        out_specs=P("lat", "lon", None),
        check_vma=False,
    )
```

```python
import functools

import jax
import jax.numpy as jnp
from jax import lax
from jax.experimental import pallas as pl
from jax.experimental.pallas import tpu as pltpu
from jax.sharding import PartitionSpec as P

HEADS = 8
HALO = 4
BF = jnp.bfloat16
F32 = jnp.float32


def silu(v):
    half = 0.5 * v
    return half + half * jnp.tanh(half)


def dot(a, b):
    return jnp.dot(a, b, preferred_element_type=F32)


def build_first_kernel(taps_ref, w1):
    cin, cout = taps_ref.shape[2:]
    w1[...] = jnp.zeros_like(w1)
    for dy in range(3):
        for col in range(4):
            for out in range(2):
                if 0 <= col - out < 3:
                    w1[dy, col * 128 : col * 128 + cin, out * cout : (out + 1) * cout] = taps_ref[
                        dy, col - out
                    ]


def turned(value):
    cin, cols = value.shape
    zeros = jnp.zeros((128 - cin, cols), F32)
    return jnp.concatenate([value.astype(F32), zeros], axis=0).T


def remote(src, dst, send, recv, lat, lon):
    return pltpu.make_async_remote_copy(
        src_ref=src, dst_ref=dst, send_sem=send, recv_sem=recv, device_id=(lat, lon),
        device_id_type=pl.DeviceIdType.MESH,
    )


def kernel(
    wide, x_ref, taps_ref, b1_ref, w2_hbm, b2_ref, w3_hbm, b3_ref, gain_ref, wqkv_hbm, sharp_ref,
    wo_hbm, out_ref, w2_ref, w3_ref, wqkv_ref, wo_ref, w1, top, bottom, edges, rims, xt, xa, first,
    second, local, whole, qs, ks, vs, att, enc, landed, weight_sem, row_sem, edge_send, edge_recv,
    go_send, go_recv, back_send, back_recv,
):
    lat, lon = lax.axis_index("lat"), lax.axis_index("lon")
    bands, sectors = lax.axis_size("lat"), lax.axis_size("lon")
    rows, cin, cols = x_ref.shape
    tokens = cols // 4
    groups = rows // 4
    has_up, has_down = lat > 0, lat < bands - 1
    up, down = jnp.maximum(lat - 1, 0), jnp.minimum(lat + 1, bands - 1)
    west, east = lax.rem(lon + sectors - 1, sectors), lax.rem(lon + 1, sectors)
    both = ((has_up, up), (has_down, down))

    weights = [
        pltpu.make_async_copy(src, dst, weight_sem.at[i])
        for i, (src, dst) in enumerate(
            ((w2_hbm, w2_ref), (w3_hbm, w3_ref), (wqkv_hbm, wqkv_ref), (wo_hbm, wo_ref))
        )
    ]

    barrier = pltpu.get_barrier_semaphore()

    def greet(to_lat, to_lon):
        pl.semaphore_signal(
            barrier, inc=1, device_id=(to_lat, to_lon), device_id_type=pl.DeviceIdType.MESH
        )

    for step in range(1, sectors):
        greet(lat, lax.rem(lon + step, sectors))
    for there, other in both:
        @pl.when(there)
        def _():
            greet(other, lon)
            greet(other, west)
            greet(other, east)

    for copy in weights:
        copy.start()
    build_first_kernel(taps_ref, w1)
    for r in range(rows + 2 * HALO):
        xt[r, 2 * HALO + cols :, :] = jnp.zeros((xt.shape[1] - cols - 2 * HALO, 128), F32)

    peers = sectors - 1 + jnp.where(has_up, 3, 0) + jnp.where(has_down, 3, 0)
    pl.semaphore_wait(barrier, peers)

    to_up = remote(x_ref.at[0:HALO], bottom, row_sem.at[0], row_sem.at[2], up, lon)
    to_down = remote(
        x_ref.at[rows - HALO : rows], top, row_sem.at[1], row_sem.at[3], down, lon
    )

    @pl.when(has_up)
    def _():
        to_up.start()

    @pl.when(has_down)
    def _():
        to_down.start()

    def own(step, carry):
        initial, last = [], []
        for k in range(4):
            r = step * 4 + k
            value = turned(x_ref[r])
            xt[r + HALO, HALO : HALO + cols, :] = value
            initial.append(value[:HALO])
            last.append(value[cols - HALO :])
        edges[0, step] = jnp.concatenate(initial, axis=0).astype(BF)
        edges[1, step] = jnp.concatenate(last, axis=0).astype(BF)
        return carry

    lax.fori_loop(0, groups, own, 0)

    rim_copies = []
    for side, to_lon in ((0, west), (1, east)):
        slot = 3 * side
        target = 1 - side
        rim_copies.append(
            (None, None, remote(
                edges.at[side], rims.at[target, pl.ds(1, groups)], edge_send.at[slot],
                edge_recv.at[slot], lat, to_lon,
            ))
        )
        rim_copies.append(
            (has_up, has_down, remote(
                edges.at[side, 0], rims.at[target, groups + 1], edge_send.at[slot + 1],
                edge_recv.at[slot + 1], up, to_lon,
            ))
        )
        rim_copies.append(
            (has_down, has_up, remote(
                edges.at[side, groups - 1], rims.at[target, 0], edge_send.at[slot + 2],
                edge_recv.at[slot + 2], down, to_lon,
            ))
        )

    def run(condition, act):
        if condition is None:
            act()
        else:
            pl.when(condition)(act)

    for sends, _, copy in rim_copies:
        run(sends, copy.start)

    @pl.when(has_up)
    def _():
        to_down.wait_recv()
        for k in range(HALO):
            xt[k, HALO : HALO + cols, :] = turned(top[k])

    @pl.when(has_down)
    def _():
        to_up.wait_recv()
        for k in range(HALO):
            xt[rows + HALO + k, HALO : HALO + cols, :] = turned(bottom[k])

    for _, receives, copy in rim_copies:
        run(receives, copy.wait_recv)

    def spread(step, carry):
        left = rims[0, step].astype(F32)
        right = rims[1, step].astype(F32)
        for k in range(4):
            r = step * 4 + k
            xt[r, 0:HALO, :] = left[k * HALO : (k + 1) * HALO]
            xt[r, HALO + cols : 2 * HALO + cols, :] = right[k * HALO : (k + 1) * HALO]
            for phase in range(6):
                part = xt[r, pl.ds(phase, wide, 4), :]
                xa[pl.ds(r * wide, wide), phase * 128 : (phase + 1) * 128] = part.astype(BF)
        return carry

    low = jnp.where(has_up, 0, 1)
    high = jnp.where(has_down, groups + 2, groups + 1)
    lax.fori_loop(low, high, spread, 0)

    @pl.when(lat == 0)
    def _():
        xa[0 : HALO * wide, :] = jnp.zeros((HALO * wide, xa.shape[1]), BF)

    @pl.when(lat == bands - 1)
    def _():
        xa[(rows + HALO) * wide :, :] = jnp.zeros((HALO * wide, xa.shape[1]), BF)

    bias1 = jnp.concatenate([b1_ref[...], b1_ref[...]], axis=1)
    kernel1 = w1[...].reshape(1536, 256)

    def conv1(step, steps):
        count = 2 * steps
        pair = []
        for side in range(2):
            lhs = jnp.concatenate(
                [
                    xa[pl.ds((2 * step + dy) * wide, count * wide), side * 256 : side * 256 + 512]
                    for dy in range(3)
                ],
                axis=1,
            )
            pair.append(silu(dot(lhs, kernel1) + bias1))
        for k in range(count):
            where = pl.ds((step + k // 2) * wide, wide)
            one = pair[0][k * wide : (k + 1) * wide]
            two = pair[1][k * wide : (k + 1) * wide]
            first[k % 2, where, 0:256] = one.astype(BF)
            first[k % 2, where, 256:512] = two.astype(BF)
            first[k % 2, where, 512:768] = pltpu.roll(one, wide - 1, 0).astype(BF)

    steps1 = (rows + 6) // 2

    def conv1_body(step, carry):
        conv1(2 * step, 2)
        return carry

    lax.fori_loop(0, steps1 // 2, conv1_body, 0)
    if steps1 % 2:
        conv1(steps1 - 1, 1)

    @pl.when(lat == 0)
    def _():
        for r in range(3):
            begin = r // 2 * wide
            first[r % 2, begin : begin + wide, :] = jnp.zeros((wide, 768), BF)

    @pl.when(lat == bands - 1)
    def _():
        for r in range(rows + 3, rows + 6):
            begin = r // 2 * wide
            first[r % 2, begin : begin + wide, :] = jnp.zeros((wide, 768), BF)

    half = rows // 2
    weights[0].wait()
    kernel2 = w2_ref[...].reshape(2048, 256)
    steps2 = (half + 2) // 2
    group = 3 if steps2 % 3 == 0 else 1
    count2 = 2 * group

    def conv2(chunk, carry):
        step = chunk * group
        for side in range(2):
            lhs = jnp.concatenate(
                [
                    first[
                        dy % 2,
                        pl.ds((2 * step + dy // 2) * wide, count2 * wide),
                        side * 256 : side * 256 + 512,
                    ]
                    for dy in range(4)
                ],
                axis=1,
            )
            result = silu(dot(lhs, kernel2) + b2_ref[...])
            for k in range(count2):
                where = pl.ds((step + k // 2) * tokens, tokens)
                a = result[k * wide : (k + 1) * wide]
                second[k % 2, where, side * 256 : side * 256 + 256] = a[:tokens].astype(BF)
                second[k % 2, where, 512 + side * 256 : 768 + side * 256] = pltpu.roll(
                    a, wide - 1, 0
                )[:tokens].astype(BF)
        return carry

    lax.fori_loop(0, steps2 // group, conv2, 0)

    @pl.when(lat == 0)
    def _():
        second[0, 0:tokens, :] = jnp.zeros((tokens, 1024), BF)

    @pl.when(lat == bands - 1)
    def _():
        begin = (half + 1) // 2 * tokens
        second[1, begin : begin + tokens, :] = jnp.zeros((tokens, 1024), BF)

    final = rows // 4
    parts = 2
    part = final // parts
    copies = max(1, sectors // final)
    each = max(1, final // sectors)
    width = w3_ref.shape[2]
    long = sectors * tokens
    share = long // copies
    weights[1].wait()

    def go(peer):
        begin = peer // copies * each
        return remote(
            local.at[pl.ds(begin, each)],
            whole.at[:, pl.ds(lon * tokens, tokens)],
            go_send.at[peer], go_recv.at[lon], lat, peer,
        )

    for step in range(parts):
        total = b3_ref[...]
        for dy in range(4):
            begin = (step * part + dy // 2) * tokens
            lhs = second[dy % 2, begin : begin + part * tokens, :]
            total = total + dot(lhs, w3_ref[dy])
        local[step * part : (step + 1) * part] = (
            silu(total).astype(BF).reshape(part, tokens, width)
        )
        for peer in range(sectors):
            if (peer // copies * each) // part == step:
                @pl.when(lon != peer)
                def _():
                    go(peer).start()

    mine_at = lon // copies * each
    whole[:, pl.ds(pl.multiple_of(lon * tokens, tokens), tokens), :] = local[
        pl.ds(mine_at, each)
    ]
    weights[2].wait()
    weights[3].wait()
    for peer in range(sectors):
        @pl.when(lon != peer)
        def _():
            remote(
                local.at[pl.ds(0, each)], whole.at[:, peer * tokens : (peer + 1) * tokens],
                go_send.at[peer], go_recv.at[peer], lat, peer,
            ).wait_recv()

    depth = width // HEADS
    lane = lax.broadcasted_iota(jnp.int32, (1, width), 1)
    scale = jnp.zeros((1, width), F32)
    for h in range(HEADS):
        inside = (lane >= h * depth) & (lane < (h + 1) * depth)
        scale = jnp.where(inside, sharp_ref[h] / jnp.sqrt(F32(depth)), scale)
    block = min(256, share)
    query_at = lax.rem(lon, copies) * share

    def back(i, peer, src_at):
        return remote(
            enc.at[i, pl.ds(src_at, tokens)], landed.at[lon // copies * each + i],
            back_send.at[i, peer], back_recv.at[i, lon], lat, peer,
        )

    for i in range(each):
        feats = whole[i].astype(F32)
        mean = jnp.mean(feats, axis=-1, keepdims=True)
        centred = feats - mean
        variance = jnp.mean(centred * centred, axis=-1, keepdims=True)
        normed = (centred * lax.rsqrt(variance + 1e-05) * gain_ref[...]).astype(BF)
        qs[i] = (dot(normed, wqkv_ref[:, :width]) * scale).astype(BF)
        ks[i] = dot(normed, wqkv_ref[:, width : 2 * width]).astype(BF)
        vs[i] = dot(normed, wqkv_ref[:, 2 * width :]).astype(BF)
        k = ks[i]
        v = vs[i]

        def attend(step, carry):
            at = pl.multiple_of(query_at + step * block, block)
            q = qs[i, pl.ds(at, block), :]
            joined = jnp.zeros((block, width), F32)
            for h in range(HEADS):
                inside = (lane >= h * depth) & (lane < (h + 1) * depth)
                masked = jnp.where(inside, q.astype(F32), 0.0).astype(BF)
                scores = lax.dot_general(
                    masked, k, (((1,), (1,)), ((), ())), preferred_element_type=F32
                )
                raised = jnp.exp(scores - jnp.max(scores, axis=-1, keepdims=True))
                total = jnp.sum(raised, axis=-1, keepdims=True)
                summed = dot(raised.astype(BF), v)
                joined = jnp.where(inside, summed / total, joined)
            mixed = dot(joined.astype(BF), wo_ref[...])
            res = whole[i, pl.ds(at, block), :].astype(F32)
            enc[i, pl.ds(at, block), :] = (res + mixed).astype(BF)
            return carry

        if share == block:
            attend(0, 0)
        else:
            lax.fori_loop(0, share // block, attend, 0)
        for peer in range(sectors):
            @pl.when((lon != peer) & (lax.rem(lon, copies) == peer * copies // sectors))
            def _():
                back(i, peer, peer * tokens).start()

        @pl.when(lax.rem(lon, copies) == lon * copies // sectors)
        def _():
            landed[lon // copies * each + i] = enc[
                i, pl.ds(pl.multiple_of(lon * tokens, tokens), tokens), :
            ]

    for i in range(each):
        for peer in range(sectors):
            @pl.when((lon != peer) & (lon * copies // sectors == peer % copies))
            def _():
                remote(
                    enc.at[i, 0:tokens], landed.at[peer // copies * each + i],
                    back_send.at[i, peer], back_recv.at[i, peer], lat, peer,
                ).wait_recv()
    out_ref[...] = landed[...]

    for sends, copy in ((has_up, to_up), (has_down, to_down)):
        run(sends, copy.wait_send)
    for sends, _, copy in rim_copies:
        run(sends, copy.wait_send)
    for peer in range(sectors):
        @pl.when(lon != peer)
        def _():
            go(peer).wait_send()
    for i in range(each):
        for peer in range(sectors):
            @pl.when((lon != peer) & (lax.rem(lon, copies) == peer * copies // sectors))
            def _():
                back(i, peer, peer * tokens).wait_send()


VM = pl.BlockSpec(memory_space=pltpu.VMEM)
SM = pl.BlockSpec(memory_space=pltpu.SMEM)
HB = pl.BlockSpec(memory_space=pl.ANY)


def on_device(x, taps1, b1, taps2, b2, taps3, b3, gain, wqkv, sharp, wo):
    rows, cin, cols = x.shape
    tokens = cols // 4
    sectors = lax.axis_size("lon")
    width = taps3.shape[3]
    wide = -(-(tokens + 2) // 16) * 16
    final = rows // 4
    each = max(1, final // sectors)
    long = sectors * tokens
    w2 = taps2.reshape(4, -1, width)
    w3 = taps3.reshape(4, -1, width)
    dma = pltpu.SemaphoreType.DMA
    return pl.pallas_call(
        functools.partial(kernel, wide),
        out_shape=jax.ShapeDtypeStruct((final, tokens, width), BF),
        in_specs=[VM, VM, VM, HB, VM, HB, VM, VM, HB, SM, HB],
        out_specs=VM,
        scratch_shapes=[
            pltpu.VMEM(w2.shape, BF),
            pltpu.VMEM(w3.shape, BF),
            pltpu.VMEM(wqkv.shape, BF),
            pltpu.VMEM(wo.shape, BF),
            pltpu.VMEM((3, 512, 256), BF),
            pltpu.VMEM((HALO, cin, cols), BF),
            pltpu.VMEM((HALO, cin, cols), BF),
            pltpu.VMEM((2, rows // 4, 16, 128), BF),
            pltpu.VMEM((2, rows // 4 + 2, 16, 128), BF),
            pltpu.VMEM((rows + 2 * HALO, 4 * wide + 8, 128), F32),
            pltpu.VMEM(((rows + 2 * HALO) * wide, 768), BF),
            pltpu.VMEM((2, (rows + 6) // 2 * wide, 768), BF),
            pltpu.VMEM((2, (rows // 2 + 2) // 2 * tokens, 1024), BF),
            pltpu.VMEM((final, tokens, width), BF),
        ]
        + [pltpu.VMEM((each, long, width), BF)] * 6
        + [
            pltpu.VMEM((final, tokens, width), BF),
            dma((4,)),
            dma((4,)),
            dma((6,)),
            dma((6,)),
            dma((sectors,)),
            dma((sectors,)),
            dma((each, sectors)),
            dma((each, sectors)),
        ],
        compiler_params=pltpu.CompilerParams(
            vmem_limit_bytes=60 * 2**20, collective_id=0, has_side_effects=True
        ),
        name="encoder",
    )(x, taps1, b1[None], w2, b2[None], w3, b3[None], gain[None], wqkv, sharp, wo)


def solution(mesh):
    return jax.shard_map(
        on_device,
        mesh=mesh,
        in_specs=(P("lat", None, "lon"), P(), P(), P(), P(), P(), P(), P(), P(), P(), P()),
        out_specs=P("lat", "lon", None),
        check_vma=False,
    )
```
